32 devices in a mesh: groups: 2 (over x), tp: 16 (over z, y, core).
Axes of the slice: x: 2, y: 2, z: 4, core: 2. Of those that a mesh axis runs over, the one named last changes fastest.
Arguments:
- queries: bfloat16 [256, 8192], P(('groups', 'tp')), parts along dimension 0, may hold values from -6 to 6
- cache_kv: bfloat16 [256, 256, 2048], P(('groups', 'tp')), parts along dimension 0, may hold values from -200 to 200
- cache_len: int32 [256], P(('groups', 'tp')), parts along dimension 0, may hold values from 2 to 256, as said below
- image_kv: bfloat16 [16384, 2048], P(('groups', 'tp')), parts along dimension 0, may hold values from -6 to 6
- row_request: int32 [16384, 1], P('groups'), parts along dimension 0, may hold values from 0 to 127; in each aligned block of 512 rows (0 to 511, 512 to 1023, ...) at most 8 rows name the same one
- slot_of_request: int32 [256], P('groups'), parts along dimension 0, may hold values from 0 to 127, each once
- out_weight: bfloat16 [8192, 8192], P('tp'), may hold values from -0.59765625 to 0.59765625
Outputs:
- projected: bfloat16 [256, 8192], P(('groups', 'tp')), parts along dimension 0
The draws below stay inside these ranges and needn't reach their ends.
There are 2 independent parts, one for each index of `groups`. The reference program is written for one: setup_inputs(seed, part) draws one part's arguments, and reference() takes and returns one part's arrays. A program takes and returns all parts, laid end to end along the dimension named above; an argument that names none is the same for every part. Nothing has to cross between parts.
Inputs may be any that keep to these rules, and one draw needn't show every extreme that they name: `row_request`: the rows of one device, 512 rows in order, name one request at most 8 times, a bound that some block reaches. `slot_of_request`: each slot once. `cache_len`: some slot holds exactly 256.
All inputs are finite; a program needn't handle non-finite values.
Results may differ from the reference program's by a relative error of at most 0.0055.
Values may be sent and summed in bfloat16 or wider, within the bound.
A program may use at most 128 MiB of HBM per device.

```python
import math
import jax
import jax.numpy as jnp
import numpy as np
from jax import lax

D = 8192
QH = 64
KVH = 8
HD = 128
CACHE = 256
IMG_DEV = 512
REQS = 128
IMG = 8192
CAP = 8
N_TP = 16


def query_values(key):
    base = jax.random.normal(jax.random.fold_in(key, 11), (REQS, D), jnp.float32)
    return jnp.clip(base, -6.0, 6.0)


def draw_queries(key, part):
    return query_values(key).astype(jnp.bfloat16)


def draw_cache_kv(key, part):
    key = jax.random.fold_in(key, 3)
    values = jax.random.normal(key, (REQS, CACHE, 2 * KVH * HD), jnp.float32)
    values = jnp.clip(values, -6.0, 6.0)
    return values.astype(jnp.bfloat16)


def draw_cache_len(key, part):
    key = jax.random.fold_in(key, 7)
    length_key, full_key = jax.random.split(key)
    lengths = jax.random.randint(length_key, (REQS,), 2, CACHE + 1)
    longest = jax.random.randint(full_key, (), 0, REQS)
    return lengths.at[longest].set(CACHE).astype(jnp.int32)


def level_of(own_key, dims, pieces, smallest, largest):
    factor_of = 1.0
    for dim, parts in pieces:
        draws = jax.random.uniform(jax.random.fold_in(jax.random.fold_in(own_key, 6), dim), (parts,), jnp.float32, smallest / len(pieces), largest / len(pieces))
        factor_of = factor_of * jnp.repeat(jnp.exp(draws), dims[dim] // parts).reshape((-1,) + (1,) * (len(dims) - 1 - dim))
    return factor_of


def routed_block(stream_key, own, number, rows, number_of, top, limit, skew):
    sequence = jax.random.permutation(stream_key, number_of)
    packed, usual = portions_of(number_of, rows * top, limit, skew, True), portions_of(number_of, rows * top, limit, skew, False)
    places = jnp.arange(number_of)

    def named(sizes, rotation):
        used = int((sizes > 0).sum())
        fixed = max(1, used // 4)
        passed = fixed + (places - fixed + rotation * (used - fixed)) % max(1, number_of - fixed)
        return jnp.zeros((number_of,), jnp.int32).at[sequence[jnp.where(places < fixed, places, passed)]].set(jnp.asarray(sizes, jnp.int32))

    sizes = jnp.where(number % 4 == 0, named(packed, number // 4), named(usual, number - number // 4 - 1))
    mixed = jax.random.permutation(jax.random.fold_in(own, 3), number_of)
    donor, sink = mixed[0:number_of // 2 * 2:2], mixed[1:number_of // 2 * 2:2]
    margin = jnp.minimum(sizes[donor] - 1, limit - sizes[sink]) // 2
    margin = jnp.where((donor == sequence[0]) | (sink == sequence[0]) | (sizes[sink] == 0), 0, jnp.maximum(margin, 0))
    passed = jax.random.randint(jax.random.fold_in(own, 4), (number_of // 2,), 0, 1 << 20) % (margin + 1)
    sizes = sizes.at[donor].add(-passed).at[sink].add(passed)
    items = jnp.searchsorted(jnp.cumsum(sizes), jnp.arange(rows * top), side="right").astype(jnp.int32)
    listing = items.reshape(top, rows).T
    listing = listing[jax.random.permutation(jax.random.fold_in(own, 1), rows)]
    rotation = jax.random.randint(jax.random.fold_in(own, 2), (rows, 1), 0, top)
    return jnp.take_along_axis(listing, (jnp.arange(top)[None, :] + rotation) % top, axis=1)


def portions_of(amount, total, most, slope, full):
    loads = [(1 << 20) // math.isqrt(rank ** slope) + 1 for rank in range(1, amount + 1)]
    largest = most if full else min(most, max(-(-total // amount), total * loads[0] // sum(loads)))
    least = 1 if total - largest >= amount - 1 else 0
    holding, spare = [largest] + [least] * (amount - 1), total - largest - least * (amount - 1)
    while spare > 0:
        free = [i for i in range(1, amount) if holding[i] < largest] or [i for i in range(1, amount) if holding[i] < most]
        pool, budget = sum([loads[i] for i in free]), spare
        for i in free:
            addition = min(most - holding[i], max(1, budget * loads[i] // pool), spare)
            holding[i] = holding[i] + addition
            spare = spare - addition
    return np.array(holding)


def normal_values(own_key, shape, width, reach, cuts=(), kind=jnp.bfloat16):
    result = jax.random.normal(own_key, shape, jnp.float32) * width
    if len(cuts) > 0:
        result = level_of(own_key, shape, cuts, -0.22, 0.18) * result
    return jnp.clip(result, min=-reach, max=reach).astype(kind)


def setup_inputs(seed: int = 0, part: int = 0) -> dict:
    key_of = jax.random.split(jax.random.key(seed), 8)
    part_keys = jax.random.split(jax.random.fold_in(key_of[7], part), 8)
    queries = draw_queries(jax.random.fold_in(jax.random.fold_in(key_of[7], part), 71), part)
    cache_kv = draw_cache_kv(jax.random.fold_in(jax.random.fold_in(key_of[7], part), 71), part)
    cache_len = draw_cache_len(jax.random.fold_in(jax.random.fold_in(key_of[7], part), 71), part)
    image_kv = normal_values(part_keys[3], (IMG, 2 * KVH * HD), 1.0, 6.0, ((0, 16),))
    row_request_keys = jax.random.split(jax.random.fold_in(part_keys[4], 1), IMG // IMG_DEV)
    row_request_turns = jax.random.permutation(jax.random.fold_in(part_keys[4], 3), IMG // IMG_DEV)
    row_request = jax.vmap(lambda own, number: routed_block(jax.random.fold_in(part_keys[4], 2), own, number, IMG_DEV, REQS, 1, CAP, 2))(row_request_keys, row_request_turns).reshape((IMG, 1))
    slot_of_request = jax.random.permutation(part_keys[5], REQS).astype(jnp.int32)
    out_weight = normal_values(key_of[6], (D, D), 0.1, 0.59765625, ((0, 16),))
    return {"queries": queries, "cache_kv": cache_kv, "cache_len": cache_len, "image_kv": image_kv, "row_request": row_request, "slot_of_request": slot_of_request, "out_weight": out_weight}


low_fill = -1e+30

def cache_terms(query_rows, cache_rows, cache_size):
    kv_width = KVH * HD
    grouped = query_rows.reshape(KVH, QH // KVH, HD).astype(jnp.float32)
    keys_all = cache_rows[:, :kv_width].reshape(CACHE, KVH, HD).astype(jnp.float32)
    vals_all = cache_rows[:, kv_width:].reshape(CACHE, KVH, HD).astype(jnp.float32)
    scores = jnp.einsum('gjd,pgd->gjp', grouped, keys_all) * (1.0 / math.sqrt(HD))
    live_mask = (jnp.arange(CACHE, dtype=jnp.int32) < cache_size)[None, None, :]
    highest = lax.optimization_barrier(jnp.max(jnp.where(live_mask, scores, low_fill), axis=-1))
    weights = jnp.where(live_mask, jnp.exp(scores - highest[..., None]), 0.0).astype(jnp.bfloat16)
    weights = lax.optimization_barrier(weights).astype(jnp.float32)
    weight_sums = lax.optimization_barrier(jnp.sum(weights, axis=-1))
    numerator = jnp.einsum('gjp,pgd->gjd', weights, vals_all)
    return (highest.reshape(QH), weight_sums.reshape(QH), numerator.reshape(QH, HD))

def reference(queries, cache_kv, cache_len, image_kv, row_request, slot_of_request, out_weight):
    kv_width = KVH * HD
    query_rows = queries.reshape(REQS, QH, HD)

    def per_slot(block_items):
        return cache_terms(block_items[0], block_items[1], block_items[2])
    top_cache, sum_cache, num_cache = lax.map(per_slot, (query_rows, cache_kv, cache_len))
    row_slot = slot_of_request[row_request[:, 0]].astype(jnp.int32)
    slot_blocks = row_slot.reshape(N_TP, IMG_DEV)
    image_blocks = image_kv.reshape(N_TP, IMG_DEV, 2 * kv_width)

    def block_scores(block_items):
        row_slots, kv_rows = block_items
        asked_rows = query_rows[row_slots].astype(jnp.float32).reshape(IMG_DEV, KVH, QH // KVH, HD)
        keys_here = kv_rows[:, :kv_width].reshape(IMG_DEV, KVH, HD).astype(jnp.float32)
        found = jnp.einsum('igjd,igd->igj', asked_rows, keys_here) * (1.0 / math.sqrt(HD))
        return found.reshape(IMG_DEV, QH)
    scores = lax.map(block_scores, (slot_blocks, image_blocks)).reshape(IMG, QH)
    image_top = jnp.full((REQS, QH), low_fill, jnp.float32).at[row_slot].max(scores)
    highest = jnp.maximum(top_cache, image_top)
    weights = jnp.exp(scores - highest[row_slot]).astype(jnp.bfloat16)
    weights = lax.optimization_barrier(weights).astype(jnp.float32)
    image_sum = jnp.zeros((REQS, QH), jnp.float32).at[row_slot].add(weights)

    def add_block(running, block_items):
        row_slots, block_weights, kv_rows = block_items
        vals_here = kv_rows[:, kv_width:].reshape(IMG_DEV, KVH, 1, HD).astype(jnp.float32)
        contribution = block_weights.reshape(IMG_DEV, KVH, QH // KVH, 1) * vals_here
        return (running.at[row_slots].add(contribution.reshape(IMG_DEV, QH, HD)), 0)
    image_num = lax.scan(add_block, jnp.zeros((REQS, QH, HD), jnp.float32), (slot_blocks, weights.reshape(N_TP, IMG_DEV, QH), image_blocks))[0]
    factor = jnp.exp(top_cache - highest)
    attended = (num_cache * factor[..., None] + image_num) / (sum_cache * factor + image_sum)[..., None]
    attended = attended.reshape(REQS, D).astype(jnp.bfloat16)
    return jnp.dot(attended, out_weight, preferred_element_type=jnp.float32).astype(jnp.bfloat16)
```

```python
import math

import jax
import jax.numpy as jnp
from jax import lax
from jax.sharding import PartitionSpec as P

QH = 64
KVH = 8
HD = 128

low_fill = -1e30


def per_device(queries, cache_kv, cache_len, image_kv, row_request, slot_of_request, out_weight):
    tp_size = lax.axis_size("tp")
    my_index = lax.axis_index("tp")
    local_req = queries.shape[0]
    cache = cache_kv.shape[1]
    all_req = local_req * tp_size
    img_local = image_kv.shape[0]
    kv_width = KVH * HD
    per_group = QH // KVH
    scale = 1.0 / math.sqrt(HD)
    all_q = lax.all_gather(queries, "tp", axis=0, tiled=True)

    grouped = queries.reshape(local_req, KVH, per_group, HD)
    cache_keys = cache_kv[:, :, :kv_width].reshape(local_req, cache, KVH, HD)
    cache_vals = cache_kv[:, :, kv_width:].reshape(local_req, cache, KVH, HD)
    cache_scores = (
        jnp.einsum("rgjd,rpgd->rgjp", grouped, cache_keys, preferred_element_type=jnp.float32) * scale
    )
    cache_live = (jnp.arange(cache, dtype=jnp.int32)[None, :] < cache_len[:, None])[:, None, None, :]
    cache_top = jnp.max(jnp.where(cache_live, cache_scores, low_fill), axis=-1)
    cache_w = jnp.where(cache_live, jnp.exp(cache_scores - cache_top[..., None]), 0.0).astype(jnp.bfloat16)
    cache_sum = jnp.sum(cache_w.astype(jnp.float32), axis=-1)
    cache_num = jnp.einsum("rgjp,rpgd->rgjd", cache_w, cache_vals, preferred_element_type=jnp.float32)

    my_rows = lax.dynamic_slice_in_dim(row_request[:, 0], my_index * img_local, img_local)
    req_iota = jnp.arange(all_req, dtype=jnp.int32)
    row_slot = jnp.sum(jnp.where(my_rows[:, None] == req_iota[None, :], slot_of_request[None, :], 0), axis=1)
    live = req_iota[:, None] == row_slot[None, :]
    img_k = image_kv[:, :kv_width].reshape(img_local, KVH, HD)
    img_v = image_kv[:, kv_width:].reshape(img_local, KVH, HD)
    qg = all_q.reshape(all_req, KVH, per_group, HD)
    s = jnp.einsum("sgjd,igd->gjsi", qg, img_k, preferred_element_type=jnp.float32) * scale
    masked = jnp.where(live[None, None], s, low_fill)
    img_top = jnp.max(masked, axis=-1)
    own_top = lax.dynamic_update_slice_in_dim(
        jnp.full((KVH, per_group, all_req), low_fill, jnp.float32),
        cache_top.transpose(1, 2, 0), my_index * local_req, 2)
    top = lax.pmax(jnp.maximum(img_top, own_top), "tp")
    w = jnp.where(live[None, None], jnp.exp(s - top[..., None]), 0.0).astype(jnp.bfloat16)
    img_sum = jnp.sum(w.astype(jnp.float32), axis=-1)
    img_num = jnp.einsum("gjsi,igd->sgjd", w, img_v, preferred_element_type=jnp.float32)
    my_top = lax.dynamic_slice_in_dim(top, my_index * local_req, local_req, 2).transpose(2, 0, 1)
    f = jnp.exp(cache_top - my_top)
    num = img_num.at[:].get()
    mine = lax.dynamic_slice_in_dim(num, my_index * local_req, local_req, 0)
    num = lax.dynamic_update_slice_in_dim(num, mine + cache_num * f[..., None], my_index * local_req, 0)
    den = img_sum.transpose(2, 0, 1)
    mine_d = lax.dynamic_slice_in_dim(den, my_index * local_req, local_req, 0)
    den = lax.dynamic_update_slice_in_dim(den, mine_d + cache_sum * f, my_index * local_req, 0)
    num = num.reshape(all_req, QH * HD)
    den = den.reshape(all_req, QH)
    num = lax.psum_scatter(num, "tp", scatter_dimension=1, tiled=True)
    den = lax.psum(den, "tp")
    hpd = QH // tp_size
    den = lax.dynamic_slice_in_dim(den, my_index * hpd, hpd, 1)
    att = (num.reshape(all_req, hpd, HD) / den[:, :, None]).astype(jnp.bfloat16).reshape(all_req, hpd * HD)
    part = jnp.dot(att, out_weight, preferred_element_type=jnp.float32)
    out = lax.psum_scatter(part, "tp", scatter_dimension=0, tiled=True)
    return out.astype(jnp.bfloat16)


def solution(mesh):
    placed = (
        P(("groups", "tp"), None),
        P(("groups", "tp"), None, None),
        P(("groups", "tp")),
        P(("groups", "tp"), None),
        P("groups", None),
        P("groups"),
        P("tp", None),
    )
    return jax.shard_map(
        per_device, mesh=mesh, in_specs=placed, out_specs=P(("groups", "tp"), None), check_vma=False
    )
```

```python
import math

import jax
import jax.numpy as jnp
from jax import lax
from jax.experimental import pallas as pl
from jax.experimental.pallas import tpu as pltpu
from jax.sharding import PartitionSpec as P
import functools

QH = 64
KVH = 8
HD = 128
CACHE = 256


low_fill = -1e30


def softmax_part(scores, live_mask, floor_top):
    masked = jnp.where(live_mask, scores, low_fill)
    highest = jnp.maximum(floor_top, jnp.max(masked, axis=-1))
    weights = jnp.where(live_mask, jnp.exp(scores - highest[..., None]), 0.0).astype(jnp.bfloat16)
    weight_sums = jnp.sum(weights.astype(jnp.float32), axis=-1)
    return (highest, weights, weight_sums)


CHUNKS = 4


def bit_of(value, bit):
    return (value // (1 << bit)) % 2


def spread(index, bits):
    total = 0
    for r, b in enumerate(bits):
        total = total + ((index // (1 << r)) % 2) * (1 << b)
    return total


def chunk_orders(n):
    bits = list(range(n.bit_length() - 1))
    first = bits
    second = bits[:1] + bits[2:] + bits[1:2]
    return [first if c % 2 == 0 else second for c in range(CHUNKS)]


def project_kernel(n, att_ref, weight_ref, out_ref, weight, got, acc, sent, landed,
                   weight_sem, att_send, att_recv, send_sem, recv_sem):
    me = lax.axis_index("tp")
    width = out_ref.shape[1] // CHUNKS
    steps = n.bit_length() - 1
    orders = chunk_orders(n)
    loads = []
    for c in range(CHUNKS):
        cols = pl.ds(c * width, width)
        load = pltpu.make_async_copy(weight_ref.at[:, cols], weight.at[:, cols], weight_sem.at[c])
        load.start()
        loads.append(load)
    barrier = pltpu.get_barrier_semaphore()

    @pl.loop(1, n)
    def _(o):
        pl.semaphore_signal(barrier, inc=1, device_id={"tp": (me + o) % n}, device_id_type=pl.DeviceIdType.MESH)

    pl.semaphore_wait(barrier, n - 1)

    def att_copy(o):
        dst = (me + o) % n
        return pltpu.make_async_remote_copy(
            src_ref=att_ref.at[dst], dst_ref=got.at[me], send_sem=att_send.at[o], recv_sem=att_recv.at[o],
            device_id={"tp": dst}, device_id_type=pl.DeviceIdType.MESH)

    @pl.loop(1, n)
    def _(o):
        att_copy(o).start()

    got[me] = att_ref[me]

    @pl.loop(1, n)
    def _(o):
        src = (me + n - o) % n
        pltpu.make_async_remote_copy(
            src_ref=att_ref.at[src], dst_ref=got.at[src], send_sem=att_send.at[o], recv_sem=att_recv.at[o],
            device_id={"tp": src}, device_id_type=pl.DeviceIdType.MESH).wait_recv()

    rows = got.shape[1]
    att = got[...].reshape(n * rows, got.shape[2]).astype(jnp.bfloat16)

    def exchange(c, k):
        m = n >> (k + 1)
        order = orders[c]
        wide = width if m > 1 else width // 2
        half = max(m // 2, 1)
        first = (n - 2 * m) // 2 if m > 1 else n // 2 - 1
        where = (pl.ds(first, half), slice(None), pl.ds(c * width, wide))
        peer = me + (1 - 2 * bit_of(me, order[k])) * (1 << order[k])
        return pltpu.make_async_remote_copy(
            src_ref=sent.at[where], dst_ref=landed.at[where], send_sem=send_sem.at[c, k], recv_sem=recv_sem.at[c, k],
            device_id={"tp": peer}, device_id_type=pl.DeviceIdType.MESH)

    def place(c, k, keep):
        order = orders[c]
        base = 0
        for b in order[:k]:
            base = base + bit_of(me, b) * (1 << b)
        own = bit_of(me, order[k])
        return base + (own if keep else 1 - own) * (1 << order[k]), order[k + 1:]

    def send(c, k):
        m = n >> (k + 1)
        base, rest = place(c, k, False)
        lo = c * width
        cols = pl.ds(lo, width)
        if m > 1:
            first = (n - 2 * m) // 2

            @pl.loop(0, m // 2)
            def _(p):
                a = base + spread(2 * p, rest)
                b = base + spread(2 * p + 1, rest)
                sent[first + p, :, cols] = jnp.concatenate([acc[a, :, cols], acc[b, :, cols]], axis=0).astype(jnp.bfloat16)
        else:
            h = width // 2
            sent[n // 2 - 1, :, pl.ds(lo, h)] = jnp.concatenate(
                [acc[base, :, pl.ds(lo, h)], acc[base, :, pl.ds(lo + h, h)]], axis=0).astype(jnp.bfloat16)
        exchange(c, k).start()

    def receive(c, k):
        m = n >> (k + 1)
        exchange(c, k).wait_recv()
        base, rest = place(c, k, True)
        lo = c * width
        cols = pl.ds(lo, width)
        if m > 1:
            first = (n - 2 * m) // 2

            @pl.loop(0, m // 2)
            def _(p):
                a = base + spread(2 * p, rest)
                b = base + spread(2 * p + 1, rest)
                both = landed[first + p, :, cols].astype(jnp.float32)
                acc[a, :, cols] = acc[a, :, cols] + both[:rows]
                acc[b, :, cols] = acc[b, :, cols] + both[rows:]
        else:
            h = width // 2
            both = landed[n // 2 - 1, :, pl.ds(lo, h)].astype(jnp.float32)
            out_ref[:, pl.ds(lo, h)] = (acc[me, :, pl.ds(lo, h)] + both[:rows]).astype(out_ref.dtype)
            out_ref[:, pl.ds(lo + h, h)] = (acc[me, :, pl.ds(lo + h, h)] + both[rows:]).astype(out_ref.dtype)

    for c in range(CHUNKS):
        loads[c].wait()
        cols = pl.ds(c * width, width)
        acc[:, :, cols] = jnp.dot(att, weight[:, cols], preferred_element_type=jnp.float32).reshape(n, rows, width)
        send(c, 0)
    for k in range(steps):
        for c in range(CHUNKS):
            receive(c, k)
            if k + 1 < steps:
                send(c, k + 1)

    @pl.loop(1, n)
    def _(o):
        att_copy(o).wait_send()

    for k in range(steps):
        for c in range(CHUNKS):
            exchange(c, k).wait_send()


def project(attended, out_weight, n):
    rows = attended.shape[0]
    model = out_weight.shape[1]
    depth = out_weight.shape[0]
    steps = n.bit_length() - 1
    by_owner = jnp.transpose(attended.reshape(rows, n, depth), (1, 0, 2))
    return pl.pallas_call(
        functools.partial(project_kernel, n),
        out_shape=jax.ShapeDtypeStruct((rows, model), jnp.bfloat16),
        in_specs=[pl.BlockSpec(memory_space=pltpu.VMEM), pl.BlockSpec(memory_space=pl.ANY)],
        out_specs=pl.BlockSpec(memory_space=pltpu.VMEM),
        scratch_shapes=[
            pltpu.VMEM((depth, model), jnp.bfloat16),
            pltpu.VMEM((n, rows, depth), jnp.float32),
            pltpu.VMEM((n, rows, model), jnp.float32),
            pltpu.VMEM((n // 2, 2 * rows, model), jnp.bfloat16),
            pltpu.VMEM((n // 2, 2 * rows, model), jnp.bfloat16),
            pltpu.SemaphoreType.DMA((CHUNKS,)),
            pltpu.SemaphoreType.DMA((n,)),
            pltpu.SemaphoreType.DMA((n,)),
            pltpu.SemaphoreType.DMA((CHUNKS, steps)),
            pltpu.SemaphoreType.DMA((CHUNKS, steps)),
        ],
        compiler_params=pltpu.CompilerParams(
            collective_id=0, has_side_effects=True, vmem_limit_bytes=48 * 1024 * 1024),
    )(by_owner, out_weight)


def per_device(queries, cache_kv, cache_len, image_kv, row_request, slot_of_request, out_weight):
    tp_size = lax.axis_size("tp")
    my_index = lax.axis_index("tp")
    local_req = queries.shape[0]
    all_req = local_req * tp_size
    img_local = image_kv.shape[0]
    kv_width = KVH * HD
    capacity = max(2, (2 * img_local + all_req - 1) // all_req)
    score_scale = 1.0 / math.sqrt(HD)
    req_iota = jnp.arange(all_req, dtype=jnp.int32)
    my_rows = lax.dynamic_slice_in_dim(row_request[:, 0], my_index * img_local, img_local)
    row_slot = jnp.sum(
        jnp.where(my_rows[:, None] == req_iota[None, :], slot_of_request[None, :], 0), axis=1
    )
    row_iota = jnp.arange(img_local, dtype=jnp.int32)
    earlier = (my_rows[:, None] == my_rows[None, :]) & (row_iota[None, :] < row_iota[:, None])
    row_rank = jnp.sum(earlier.astype(jnp.int32), axis=1)
    bucket = jnp.zeros((all_req * capacity, 2 * kv_width), jnp.bfloat16)
    bucket = bucket.at[row_slot * capacity + row_rank].set(image_kv)
    bucket = bucket.reshape(all_req, capacity, 2 * kv_width)
    arrived = lax.all_to_all(bucket, "tp", split_axis=0, concat_axis=1, tiled=True)
    grouped = queries.reshape(local_req, KVH, QH // KVH, HD)
    cache_keys = cache_kv[:, :, :kv_width].reshape(local_req, CACHE, KVH, HD)
    cache_vals = cache_kv[:, :, kv_width:].reshape(local_req, CACHE, KVH, HD)
    cache_scores = (
        jnp.einsum("rgjd,rpgd->rgjp", grouped, cache_keys, preferred_element_type=jnp.float32)
        * score_scale
    )
    cache_live = (jnp.arange(CACHE, dtype=jnp.int32)[None, :] < cache_len[:, None])[
        :, None, None, :
    ]
    cache_top, cache_weights, cache_sum = softmax_part(cache_scores, cache_live, low_fill)
    cache_num = jnp.einsum(
        "rgjp,rpgd->rgjd", cache_weights, cache_vals, preferred_element_type=jnp.float32
    )
    my_slots = my_index * local_req + jnp.arange(local_req, dtype=jnp.int32)
    owned_slot = slot_of_request[:, None] == my_slots[None, :]
    my_requests = jnp.sum(jnp.where(owned_slot, req_iota[:, None], 0), axis=0)
    matches = (row_request[:, 0][:, None] == my_requests[None, :]).astype(jnp.int32)
    counts = jnp.sum(matches.reshape(tp_size, img_local, local_req), axis=1)
    rank_iota = jnp.arange(capacity, dtype=jnp.int32)
    image_live = rank_iota[None, :, None] < counts[:, None, :]
    image_live = jnp.transpose(image_live, (2, 0, 1)).reshape(local_req, tp_size * capacity)[
        :, None, None, :
    ]
    image_keys = arrived[:, :, :kv_width].reshape(local_req, tp_size * capacity, KVH, HD)
    image_vals = arrived[:, :, kv_width:].reshape(local_req, tp_size * capacity, KVH, HD)
    image_scores = (
        jnp.einsum("rgjd,rsgd->rgjs", grouped, image_keys, preferred_element_type=jnp.float32)
        * score_scale
    )
    image_top, image_weights, image_sum = softmax_part(image_scores, image_live, cache_top)
    image_num = jnp.einsum(
        "rgjs,rsgd->rgjd", image_weights, image_vals, preferred_element_type=jnp.float32
    )
    factor = jnp.exp(cache_top - image_top)
    attended = (cache_num * factor[..., None] + image_num) / (cache_sum * factor + image_sum)[
        ..., None
    ]
    return project(attended.reshape(local_req, QH * HD), out_weight, tp_size)


def solution(mesh):
    placed = (
        P(("groups", "tp"), None),
        P(("groups", "tp"), None, None),
        P(("groups", "tp")),
        P(("groups", "tp"), None),
        P("groups", None),
        P("groups"),
        P("tp", None),
    )
    return jax.shard_map(
        per_device, mesh=mesh, in_specs=placed, out_specs=P(("groups", "tp"), None), check_vma=False
    )
```

```python
import math

import jax
import jax.numpy as jnp
from jax import lax
from jax.experimental import pallas as pl
from jax.experimental.pallas import tpu as pltpu
from jax.sharding import PartitionSpec as P
import functools

QH = 64
KVH = 8
HD = 128
CACHE = 256


low_fill = -1e30


def softmax_part(scores, live_mask, floor_top):
    masked = jnp.where(live_mask, scores, low_fill)
    highest = jnp.maximum(floor_top, jnp.max(masked, axis=-1))
    weights = jnp.where(live_mask, jnp.exp(scores - highest[..., None]), 0.0).astype(jnp.bfloat16)
    weight_sums = jnp.sum(weights.astype(jnp.float32), axis=-1)
    return (highest, weights, weight_sums)


CHUNKS = 4


def bit_of(value, bit):
    return (value // (1 << bit)) % 2


def spread(index, bits):
    total = 0
    for r, b in enumerate(bits):
        total = total + ((index // (1 << r)) % 2) * (1 << b)
    return total


def chunk_orders(n):
    bits = list(range(n.bit_length() - 1))
    first = bits
    second = bits[:1] + bits[2:] + bits[1:2]
    return [first if c % 2 == 0 else second for c in range(CHUNKS)]


def image_heads(n, query_ref, image_ref, bias_ref, num, stat):
    per_dev = QH // n
    per_chunk = per_dev // 2
    per_group = QH // KVH
    stat[...] = jnp.zeros_like(stat)

    @pl.loop(0, KVH)
    def _(g):
        keys = image_ref[:, pl.ds(pl.multiple_of(g * HD, HD), HD)]
        vals = image_ref[:, pl.ds(pl.multiple_of((KVH + g) * HD, HD), HD)].T
        for j in range(per_group):
            q = query_ref[:, pl.ds(pl.multiple_of((g * per_group + j) * HD, HD), HD)]
            s = lax.dot_general(keys, q, (((1,), (1,)), ((), ())), preferred_element_type=jnp.float32)
            s = s * (1.0 / math.sqrt(HD)) + bias_ref[...]
            top = jnp.maximum(jnp.max(s, axis=0, keepdims=True), 0.1 * low_fill)
            w = jnp.exp(s - top).astype(jnp.bfloat16)
            dst = g * (per_group // per_dev) + j // per_dev
            c, i = (j % per_dev) // per_chunk, j % per_chunk
            num[c, dst, pl.ds(i * HD, HD), :] = jnp.dot(vals, w, preferred_element_type=jnp.float32)
            stat[c, dst, pl.ds(i, 1), :] = top
            stat[c, dst, pl.ds(4 + i, 1), :] = jnp.sum(w.astype(jnp.float32), axis=0, keepdims=True)


def sum_heads(n, num, stat, num_sent, num_got, stat_sent, stat_got, send_sem, recv_sem):
    me = lax.axis_index("tp")
    steps = n.bit_length() - 1
    per_chunk = QH // n // 2

    def copies(c, k):
        m = n >> (k + 1)
        order = chunk_orders(n)[c]
        peer = me + (1 - 2 * bit_of(me, order[k])) * (1 << order[k])
        at = pl.ds(n - 2 * m, m)
        return [pltpu.make_async_remote_copy(
            src_ref=a.at[c, at], dst_ref=b.at[c, at], send_sem=send_sem.at[c, k, i], recv_sem=recv_sem.at[c, k, i],
            device_id={"tp": peer}, device_id_type=pl.DeviceIdType.MESH)
            for i, (a, b) in enumerate([(stat_sent, stat_got), (num_sent, num_got)])]

    def place(c, k, keep):
        order = chunk_orders(n)[c]
        base = 0
        for b in order[:k]:
            base = base + bit_of(me, b) * (1 << b)
        own = bit_of(me, order[k])
        return base + (own if keep else 1 - own) * (1 << order[k]), order[k + 1:]

    def send(c, k):
        m = n >> (k + 1)
        base, rest = place(c, k, False)

        @pl.loop(0, m)
        def _(p):
            d = base + spread(p, rest)
            num_sent[c, n - 2 * m + p] = num[c, d].astype(jnp.bfloat16)
            stat_sent[c, n - 2 * m + p] = stat[c, d]

        for copy in copies(c, k):
            copy.start()

    def receive(c, k):
        m = n >> (k + 1)
        base, rest = place(c, k, True)
        for copy in copies(c, k):
            copy.wait_recv()

        @pl.loop(0, m)
        def _(p):
            d = base + spread(p, rest)
            for i in range(per_chunk):
                ta, tb = stat[c, d, pl.ds(i, 1), :], stat_got[c, n - 2 * m + p, pl.ds(i, 1), :]
                sa, sb = stat[c, d, pl.ds(4 + i, 1), :], stat_got[c, n - 2 * m + p, pl.ds(4 + i, 1), :]
                top = jnp.maximum(ta, tb)
                ea, eb = jnp.exp(ta - top), jnp.exp(tb - top)
                part = pl.ds(i * HD, HD)
                other = num_got[c, n - 2 * m + p, part, :].astype(jnp.float32)
                num[c, d, part, :] = num[c, d, part, :] * ea + other * eb
                stat[c, d, pl.ds(i, 1), :] = top
                stat[c, d, pl.ds(4 + i, 1), :] = sa * ea + sb * eb

    for c in range(2):
        send(c, 0)
    for k in range(steps):
        for c in range(2):
            receive(c, k)
            if k + 1 < steps:
                send(c, k + 1)
    return [copy for k in range(steps) for c in range(2) for copy in copies(c, k)]


def project_kernel(n, fused, *refs):
    if fused:
        (att_ref, weight_ref, query_ref, image_ref, bias_ref, out_ref, weight, got, acc, sent, landed,
         weight_sem, att_send, att_recv, send_sem, recv_sem,
         num, stat, num_sent, num_got, stat_sent, stat_got, head_send, head_recv) = refs
    else:
        (att_ref, weight_ref, out_ref, weight, got, acc, sent, landed,
         weight_sem, att_send, att_recv, send_sem, recv_sem) = refs
    me = lax.axis_index("tp")
    width = out_ref.shape[1] // CHUNKS
    steps = n.bit_length() - 1
    orders = chunk_orders(n)
    loads = []
    for c in range(CHUNKS):
        cols = pl.ds(c * width, width)
        load = pltpu.make_async_copy(weight_ref.at[:, cols], weight.at[:, cols], weight_sem.at[c])
        load.start()
        loads.append(load)
    barrier = pltpu.get_barrier_semaphore()

    @pl.loop(1, n)
    def _(o):
        pl.semaphore_signal(barrier, inc=1, device_id={"tp": (me + o) % n}, device_id_type=pl.DeviceIdType.MESH)

    pl.semaphore_wait(barrier, n - 1)

    def att_copy(o):
        dst = (me + o) % n
        return pltpu.make_async_remote_copy(
            src_ref=att_ref.at[dst], dst_ref=got.at[me], send_sem=att_send.at[o], recv_sem=att_recv.at[o],
            device_id={"tp": dst}, device_id_type=pl.DeviceIdType.MESH)

    @pl.loop(1, n)
    def _(o):
        att_copy(o).start()

    got[me] = att_ref[me]
    started = []
    if fused:
        image_heads(n, query_ref, image_ref, bias_ref, num, stat)
        started = sum_heads(n, num, stat, num_sent, num_got, stat_sent, stat_got, head_send, head_recv)

    @pl.loop(1, n)
    def _(o):
        src = (me + n - o) % n
        pltpu.make_async_remote_copy(
            src_ref=att_ref.at[src], dst_ref=got.at[src], send_sem=att_send.at[o], recv_sem=att_recv.at[o],
            device_id={"tp": src}, device_id_type=pl.DeviceIdType.MESH).wait_recv()

    rows = got.shape[1]
    if fused:
        per_dev = QH // n
        cached = got[...].reshape(n * rows, got.shape[2]).T
        depth = per_dev * HD
        pieces = []
        for h in range(per_dev):
            c, i = h // (per_dev // 2), h % (per_dev // 2)
            ct, cs = cached[depth + h:depth + h + 1], cached[depth + 64 + h:depth + 65 + h]
            it, isum = stat[c, me, pl.ds(i, 1), :], stat[c, me, pl.ds(4 + i, 1), :]
            top = jnp.maximum(ct, it)
            ce, ie = jnp.exp(ct - top), jnp.exp(it - top)
            total = cached[h * HD:(h + 1) * HD] * ce + num[c, me, pl.ds(i * HD, HD), :] * ie
            pieces.append((total / (cs * ce + isum * ie)).T)
        att = jnp.concatenate(pieces, axis=1).astype(jnp.bfloat16)
    else:
        att = got[...].reshape(n * rows, got.shape[2]).astype(jnp.bfloat16)

    def exchange(c, k):
        m = n >> (k + 1)
        order = orders[c]
        wide = width if m > 1 else width // 2
        half = max(m // 2, 1)
        first = (n - 2 * m) // 2 if m > 1 else n // 2 - 1
        where = (pl.ds(first, half), slice(None), pl.ds(c * width, wide))
        peer = me + (1 - 2 * bit_of(me, order[k])) * (1 << order[k])
        return pltpu.make_async_remote_copy(
            src_ref=sent.at[where], dst_ref=landed.at[where], send_sem=send_sem.at[c, k], recv_sem=recv_sem.at[c, k],
            device_id={"tp": peer}, device_id_type=pl.DeviceIdType.MESH)

    def place(c, k, keep):
        order = orders[c]
        base = 0
        for b in order[:k]:
            base = base + bit_of(me, b) * (1 << b)
        own = bit_of(me, order[k])
        return base + (own if keep else 1 - own) * (1 << order[k]), order[k + 1:]

    def send(c, k):
        m = n >> (k + 1)
        base, rest = place(c, k, False)
        lo = c * width
        cols = pl.ds(lo, width)
        if m > 1:
            first = (n - 2 * m) // 2

            @pl.loop(0, m // 2)
            def _(p):
                a = base + spread(2 * p, rest)
                b = base + spread(2 * p + 1, rest)
                sent[first + p, :, cols] = jnp.concatenate([acc[a, :, cols], acc[b, :, cols]], axis=0).astype(jnp.bfloat16)
        else:
            h = width // 2
            sent[n // 2 - 1, :, pl.ds(lo, h)] = jnp.concatenate(
                [acc[base, :, pl.ds(lo, h)], acc[base, :, pl.ds(lo + h, h)]], axis=0).astype(jnp.bfloat16)
        exchange(c, k).start()

    def receive(c, k):
        m = n >> (k + 1)
        exchange(c, k).wait_recv()
        base, rest = place(c, k, True)
        lo = c * width
        cols = pl.ds(lo, width)
        if m > 1:
            first = (n - 2 * m) // 2

            @pl.loop(0, m // 2)
            def _(p):
                a = base + spread(2 * p, rest)
                b = base + spread(2 * p + 1, rest)
                both = landed[first + p, :, cols].astype(jnp.float32)
                acc[a, :, cols] = acc[a, :, cols] + both[:rows]
                acc[b, :, cols] = acc[b, :, cols] + both[rows:]
        else:
            h = width // 2
            both = landed[n // 2 - 1, :, pl.ds(lo, h)].astype(jnp.float32)
            out_ref[:, pl.ds(lo, h)] = (acc[me, :, pl.ds(lo, h)] + both[:rows]).astype(out_ref.dtype)
            out_ref[:, pl.ds(lo + h, h)] = (acc[me, :, pl.ds(lo + h, h)] + both[rows:]).astype(out_ref.dtype)

    for c in range(CHUNKS):
        loads[c].wait()
        cols = pl.ds(c * width, width)
        acc[:, :, cols] = jnp.dot(att, weight[:, cols], preferred_element_type=jnp.float32).reshape(n, rows, width)
        send(c, 0)
    for k in range(steps):
        for c in range(CHUNKS):
            receive(c, k)
            if k + 1 < steps:
                send(c, k + 1)

    @pl.loop(1, n)
    def _(o):
        att_copy(o).wait_send()

    for copy in started:
        copy.wait_send()
    for k in range(steps):
        for c in range(CHUNKS):
            exchange(c, k).wait_send()


def project(by_owner, out_weight, n, image=()):
    rows = by_owner.shape[1]
    model = out_weight.shape[1]
    depth = out_weight.shape[0]
    steps = n.bit_length() - 1
    extra = []
    if image:
        half = depth // 2
        every = n * rows
        extra = [
            pltpu.VMEM((2, n, half, every), jnp.float32),
            pltpu.VMEM((2, n, 8, every), jnp.float32),
            pltpu.VMEM((2, n - 1, half, every), jnp.bfloat16),
            pltpu.VMEM((2, n - 1, half, every), jnp.bfloat16),
            pltpu.VMEM((2, n - 1, 8, every), jnp.float32),
            pltpu.VMEM((2, n - 1, 8, every), jnp.float32),
            pltpu.SemaphoreType.DMA((2, steps, 2)),
            pltpu.SemaphoreType.DMA((2, steps, 2)),
        ]
    return pl.pallas_call(
        functools.partial(project_kernel, n, bool(image)),
        out_shape=jax.ShapeDtypeStruct((rows, model), jnp.bfloat16),
        in_specs=[pl.BlockSpec(memory_space=pltpu.VMEM), pl.BlockSpec(memory_space=pl.ANY)]
        + [pl.BlockSpec(memory_space=pltpu.VMEM)] * len(image),
        out_specs=pl.BlockSpec(memory_space=pltpu.VMEM),
        scratch_shapes=[
            pltpu.VMEM((depth, model), jnp.bfloat16),
            pltpu.VMEM(by_owner.shape, jnp.float32),
            pltpu.VMEM((n, rows, model), jnp.float32),
            pltpu.VMEM((n // 2, 2 * rows, model), jnp.bfloat16),
            pltpu.VMEM((n // 2, 2 * rows, model), jnp.bfloat16),
            pltpu.SemaphoreType.DMA((CHUNKS,)),
            pltpu.SemaphoreType.DMA((n,)),
            pltpu.SemaphoreType.DMA((n,)),
            pltpu.SemaphoreType.DMA((CHUNKS, steps)),
            pltpu.SemaphoreType.DMA((CHUNKS, steps)),
        ] + extra,
        compiler_params=pltpu.CompilerParams(
            collective_id=0, has_side_effects=True, vmem_limit_bytes=48 * 1024 * 1024),
    )(by_owner, out_weight, *image)


def per_device(queries, cache_kv, cache_len, image_kv, row_request, slot_of_request, out_weight):
    tp_size = lax.axis_size("tp")
    my_index = lax.axis_index("tp")
    local_req = queries.shape[0]
    all_req = local_req * tp_size
    img_local = image_kv.shape[0]
    kv_width = KVH * HD
    capacity = max(2, (2 * img_local + all_req - 1) // all_req)
    score_scale = 1.0 / math.sqrt(HD)
    req_iota = jnp.arange(all_req, dtype=jnp.int32)
    my_rows = lax.dynamic_slice_in_dim(row_request[:, 0], my_index * img_local, img_local)
    row_slot = jnp.sum(
        jnp.where(my_rows[:, None] == req_iota[None, :], slot_of_request[None, :], 0), axis=1
    )
    grouped = queries.reshape(local_req, KVH, QH // KVH, HD)
    cache_keys = cache_kv[:, :, :kv_width].reshape(local_req, CACHE, KVH, HD)
    cache_vals = cache_kv[:, :, kv_width:].reshape(local_req, CACHE, KVH, HD)
    cache_scores = (
        jnp.einsum("rgjd,rpgd->rgjp", grouped, cache_keys, preferred_element_type=jnp.float32)
        * score_scale
    )
    cache_live = (jnp.arange(CACHE, dtype=jnp.int32)[None, :] < cache_len[:, None])[
        :, None, None, :
    ]
    cache_top, cache_weights, cache_sum = softmax_part(cache_scores, cache_live, low_fill)
    cache_num = jnp.einsum(
        "rgjp,rpgd->rgjd", cache_weights, cache_vals, preferred_element_type=jnp.float32
    )
    per_dev = QH // tp_size
    if per_dev % 2 == 0 and per_dev <= QH // KVH:
        live = row_slot[:, None] == req_iota[None, :]
        bias = jnp.where(live, 0.0, low_fill).astype(jnp.float32)
        every = lax.all_gather(queries, "tp", axis=0, tiled=True)

        def spare(x):
            x = x.reshape(local_req, tp_size, per_dev)
            return jnp.pad(x, ((0, 0), (0, 0), (0, 64 - per_dev)))

        packed = jnp.concatenate(
            [cache_num.reshape(local_req, tp_size, per_dev * HD), spare(cache_top), spare(cache_sum)], axis=2)
        return project(jnp.transpose(packed, (1, 0, 2)), out_weight, tp_size, (every, image_kv, bias))
    row_iota = jnp.arange(img_local, dtype=jnp.int32)
    earlier = (my_rows[:, None] == my_rows[None, :]) & (row_iota[None, :] < row_iota[:, None])
    row_rank = jnp.sum(earlier.astype(jnp.int32), axis=1)
    bucket = jnp.zeros((all_req * capacity, 2 * kv_width), jnp.bfloat16)
    bucket = bucket.at[row_slot * capacity + row_rank].set(image_kv)
    bucket = bucket.reshape(all_req, capacity, 2 * kv_width)
    arrived = lax.all_to_all(bucket, "tp", split_axis=0, concat_axis=1, tiled=True)
    my_slots = my_index * local_req + jnp.arange(local_req, dtype=jnp.int32)
    owned_slot = slot_of_request[:, None] == my_slots[None, :]
    my_requests = jnp.sum(jnp.where(owned_slot, req_iota[:, None], 0), axis=0)
    matches = (row_request[:, 0][:, None] == my_requests[None, :]).astype(jnp.int32)
    counts = jnp.sum(matches.reshape(tp_size, img_local, local_req), axis=1)
    rank_iota = jnp.arange(capacity, dtype=jnp.int32)
    image_live = rank_iota[None, :, None] < counts[:, None, :]
    image_live = jnp.transpose(image_live, (2, 0, 1)).reshape(local_req, tp_size * capacity)[
        :, None, None, :
    ]
    image_keys = arrived[:, :, :kv_width].reshape(local_req, tp_size * capacity, KVH, HD)
    image_vals = arrived[:, :, kv_width:].reshape(local_req, tp_size * capacity, KVH, HD)
    image_scores = (
        jnp.einsum("rgjd,rsgd->rgjs", grouped, image_keys, preferred_element_type=jnp.float32)
        * score_scale
    )
    image_top, image_weights, image_sum = softmax_part(image_scores, image_live, cache_top)
    image_num = jnp.einsum(
        "rgjs,rsgd->rgjd", image_weights, image_vals, preferred_element_type=jnp.float32
    )
    factor = jnp.exp(cache_top - image_top)
    attended = (cache_num * factor[..., None] + image_num) / (cache_sum * factor + image_sum)[
        ..., None
    ]
    by_owner = jnp.transpose(attended.reshape(local_req, tp_size, QH * HD // tp_size), (1, 0, 2))
    return project(by_owner, out_weight, tp_size)


def solution(mesh):
    placed = (
        P(("groups", "tp"), None),
        P(("groups", "tp"), None, None),
        P(("groups", "tp")),
        P(("groups", "tp"), None),
        P("groups", None),
        P("groups"),
        P("tp", None),
    )
    return jax.shard_map(
        per_device, mesh=mesh, in_specs=placed, out_specs=P(("groups", "tp"), None), check_vma=False
    )
```

```python
import math

import jax
import jax.numpy as jnp
from jax import lax
from jax.experimental import pallas as pl
from jax.experimental.pallas import tpu as pltpu
from jax.sharding import PartitionSpec as P
import functools

QH = 64
KVH = 8
HD = 128
CACHE = 256


low_fill = -1e30


def softmax_part(scores, live_mask, floor_top):
    masked = jnp.where(live_mask, scores, low_fill)
    highest = jnp.maximum(floor_top, jnp.max(masked, axis=-1))
    weights = jnp.where(live_mask, jnp.exp(scores - highest[..., None]), 0.0).astype(jnp.bfloat16)
    weight_sums = jnp.sum(weights.astype(jnp.float32), axis=-1)
    return (highest, weights, weight_sums)


CHUNKS = 4


def bit_of(value, bit):
    return (value // (1 << bit)) % 2


def spread(index, bits):
    total = 0
    for r, b in enumerate(bits):
        total = total + ((index // (1 << r)) % 2) * (1 << b)
    return total


def chunk_orders(n):
    bits = list(range(n.bit_length() - 1))
    first = bits
    second = bits[:1] + bits[2:] + bits[1:2]
    return [first if c % 2 == 0 else second for c in range(CHUNKS)]


def image_heads(n, query_ref, image_ref, bias_ref, num, stat):
    per_dev = QH // n
    per_chunk = per_dev // 2
    per_group = QH // KVH
    stat[...] = jnp.zeros_like(stat)

    @pl.loop(0, KVH)
    def _(g):
        keys = image_ref[:, pl.ds(pl.multiple_of(g * HD, HD), HD)]
        vals = image_ref[:, pl.ds(pl.multiple_of((KVH + g) * HD, HD), HD)].T
        pairs = []
        for j in range(per_group // 2):
            cols = pl.ds(pl.multiple_of((g * (per_group // 2) + j) * HD, HD), HD)
            both = query_ref[:, :, cols].astype(jnp.float32)
            rows = both.shape[1] // 2
            pairs.append([both[:, h * rows:(h + 1) * rows].reshape(n * rows, HD).astype(jnp.bfloat16) for h in (0, 1)])
        for j in range(per_group):
            q = pairs[j % (per_group // 2)][j // (per_group // 2)]
            s = lax.dot_general(keys, q, (((1,), (1,)), ((), ())), preferred_element_type=jnp.float32)
            s = s * (1.0 / math.sqrt(HD)) + bias_ref[...]
            top = jnp.maximum(jnp.max(s, axis=0, keepdims=True), 0.1 * low_fill)
            w = jnp.exp(s - top).astype(jnp.bfloat16)
            dst = g * (per_group // per_dev) + j // per_dev
            c, i = (j % per_dev) // per_chunk, j % per_chunk
            num[c, dst, pl.ds(i * HD, HD), :] = jnp.dot(vals, w, preferred_element_type=jnp.float32)
            stat[c, dst, pl.ds(i, 1), :] = top
            stat[c, dst, pl.ds(4 + i, 1), :] = jnp.sum(w.astype(jnp.float32), axis=0, keepdims=True)


def sum_heads(n, num, stat, num_sent, num_got, stat_sent, stat_got, send_sem, recv_sem):
    me = lax.axis_index("tp")
    steps = n.bit_length() - 1
    per_chunk = QH // n // 2

    def copies(c, k):
        m = n >> (k + 1)
        order = chunk_orders(n)[c]
        peer = me + (1 - 2 * bit_of(me, order[k])) * (1 << order[k])
        at = pl.ds(n - 2 * m, m)
        return [pltpu.make_async_remote_copy(
            src_ref=a.at[c, at], dst_ref=b.at[c, at], send_sem=send_sem.at[c, k, i], recv_sem=recv_sem.at[c, k, i],
            device_id={"tp": peer}, device_id_type=pl.DeviceIdType.MESH)
            for i, (a, b) in enumerate([(stat_sent, stat_got), (num_sent, num_got)])]

    def place(c, k, keep):
        order = chunk_orders(n)[c]
        base = 0
        for b in order[:k]:
            base = base + bit_of(me, b) * (1 << b)
        own = bit_of(me, order[k])
        return base + (own if keep else 1 - own) * (1 << order[k]), order[k + 1:]

    def send(c, k):
        m = n >> (k + 1)
        base, rest = place(c, k, False)

        @pl.loop(0, m)
        def _(p):
            d = base + spread(p, rest)
            num_sent[c, n - 2 * m + p] = num[c, d].astype(jnp.bfloat16)
            stat_sent[c, n - 2 * m + p] = stat[c, d]

        for copy in copies(c, k):
            copy.start()

    def receive(c, k):
        m = n >> (k + 1)
        base, rest = place(c, k, True)
        for copy in copies(c, k):
            copy.wait_recv()

        @pl.loop(0, m)
        def _(p):
            d = base + spread(p, rest)
            for i in range(per_chunk):
                ta, tb = stat[c, d, pl.ds(i, 1), :], stat_got[c, n - 2 * m + p, pl.ds(i, 1), :]
                sa, sb = stat[c, d, pl.ds(4 + i, 1), :], stat_got[c, n - 2 * m + p, pl.ds(4 + i, 1), :]
                top = jnp.maximum(ta, tb)
                ea, eb = jnp.exp(ta - top), jnp.exp(tb - top)
                part = pl.ds(i * HD, HD)
                other = num_got[c, n - 2 * m + p, part, :].astype(jnp.float32)
                num[c, d, part, :] = num[c, d, part, :] * ea + other * eb
                stat[c, d, pl.ds(i, 1), :] = top
                stat[c, d, pl.ds(4 + i, 1), :] = sa * ea + sb * eb

    for c in range(2):
        send(c, 0)
    for k in range(steps):
        for c in range(2):
            receive(c, k)
            if k + 1 < steps:
                send(c, k + 1)
    return [copy for k in range(steps) for c in range(2) for copy in copies(c, k)]


def cache_slot(n, r, heads_ref, cache, live_ref, att):
    per_dev = QH // n
    per_group = QH // KVH
    lane = lax.broadcasted_iota(jnp.int32, (per_group, HD), 1)
    head = lax.broadcasted_iota(jnp.int32, (per_group, HD), 0) % per_dev
    for g in range(KVH):
        q = heads_ref[r, pl.ds(g * per_group, per_group), :].astype(jnp.bfloat16)
        s = lax.dot_general(q, cache[r, :, pl.ds(g * HD, HD)], (((1,), (1,)), ((), ())),
                            preferred_element_type=jnp.float32)
        s = s * (1.0 / math.sqrt(HD)) + live_ref[pl.ds(r, 1), :]
        top = jnp.max(s, axis=1, keepdims=True)
        w = jnp.exp(s - top).astype(jnp.bfloat16)
        total = jnp.sum(w.astype(jnp.float32), axis=1, keepdims=True)
        part = jnp.dot(w, cache[r, :, pl.ds((KVH + g) * HD, HD)], preferred_element_type=jnp.float32)
        stats = jnp.where(lane == head, top, 0.0) + jnp.where(lane == head + 64, total, 0.0)
        for d in range(per_group // per_dev):
            dst = g * (per_group // per_dev) + d
            for i in range(per_dev):
                at = d * per_dev + i
                att[dst, i, pl.ds(r, 1), :] = part[at:at + 1]
            att[dst, per_dev, pl.ds(r, 1), :] = jnp.sum(
                stats[d * per_dev:(d + 1) * per_dev], axis=0, keepdims=True)


def gather_copies(n, c, k, query_ref, every, send_sem, recv_sem):
    me = lax.axis_index("tp")
    bits = list(range(n.bit_length() - 1))
    order = bits[:0:-1] + bits[:1] if c == 0 else bits[1:2] + bits[:1:-1] + bits[:1]
    base = me
    for b in order[:k]:
        base = base - bit_of(me, b) * (1 << b)
    peer = me + (1 - 2 * bit_of(me, order[k])) * (1 << order[k])
    wide = every.shape[2] // 2
    cols = pl.ds(c * wide, wide)
    copies = []
    for j in range(1 << k):
        at = base + sum([((j >> i) & 1) * (1 << b) for i, b in enumerate(order[:k])])
        slot = (1 << k) - 1 + j
        copies.append(pltpu.make_async_remote_copy(
            src_ref=query_ref.at[:, cols] if k == 0 else every.at[at, :, cols], dst_ref=every.at[at, :, cols],
            send_sem=send_sem.at[c, slot], recv_sem=recv_sem.at[c, slot],
            device_id={"tp": peer}, device_id_type=pl.DeviceIdType.MESH))
    return copies


def project_kernel(n, fused, *refs):
    if fused:
        (query_ref, weight_ref, heads_ref, cache_ref, live_ref, image_ref, bias_ref, out_ref, weight, got, acc, sent, landed,
         weight_sem, att_send, att_recv, send_sem, recv_sem,
         num, stat, num_sent, num_got, stat_sent, stat_got, head_send, head_recv,
         att_ref, every, cache, cache_sem, query_send, query_recv) = refs
    else:
        (att_ref, weight_ref, out_ref, weight, got, acc, sent, landed,
         weight_sem, att_send, att_recv, send_sem, recv_sem) = refs
    me = lax.axis_index("tp")
    width = out_ref.shape[1] // CHUNKS
    steps = n.bit_length() - 1
    orders = chunk_orders(n)
    rows = out_ref.shape[0]
    if fused:
        def cache_load(r):
            return pltpu.make_async_copy(cache_ref.at[r], cache.at[r], cache_sem.at[r])

        @pl.loop(0, rows)
        def _(r):
            cache_load(r).start()
    loads = []
    for c in range(CHUNKS):
        cols = pl.ds(c * width, width)
        load = pltpu.make_async_copy(weight_ref.at[:, cols], weight.at[:, cols], weight_sem.at[c])
        load.start()
        loads.append(load)
    barrier = pltpu.get_barrier_semaphore()

    @pl.loop(1, n)
    def _(o):
        pl.semaphore_signal(barrier, inc=1, device_id={"tp": (me + o) % n}, device_id_type=pl.DeviceIdType.MESH)

    pl.semaphore_wait(barrier, n - 1)

    def att_copy(o):
        dst = (me + o) % n
        return pltpu.make_async_remote_copy(
            src_ref=att_ref.at[dst], dst_ref=got.at[me], send_sem=att_send.at[o], recv_sem=att_recv.at[o],
            device_id={"tp": dst}, device_id_type=pl.DeviceIdType.MESH)

    started = []
    if fused:
        every[me] = query_ref[...]
        per_step = -(-rows // steps)
        for k in range(steps):
            for c in range(2):
                copies = gather_copies(n, c, k, query_ref, every, query_send, query_recv)
                for copy in copies:
                    copy.start()
                started = started + copies

            @pl.loop(min(rows, k * per_step), min(rows, (k + 1) * per_step))
            def _(r):
                cache_load(r).wait()
                cache_slot(n, r, heads_ref, cache, live_ref, att_ref)

            for c in range(2):
                for copy in gather_copies(n, c, k, query_ref, every, query_send, query_recv):
                    copy.wait_recv()

    @pl.loop(1, n)
    def _(o):
        att_copy(o).start()

    got[me] = att_ref[me]
    if fused:
        image_heads(n, every, image_ref, bias_ref, num, stat)
        started = started + sum_heads(n, num, stat, num_sent, num_got, stat_sent, stat_got, head_send, head_recv)

    @pl.loop(1, n)
    def _(o):
        src = (me + n - o) % n
        pltpu.make_async_remote_copy(
            src_ref=att_ref.at[src], dst_ref=got.at[src], send_sem=att_send.at[o], recv_sem=att_recv.at[o],
            device_id={"tp": src}, device_id_type=pl.DeviceIdType.MESH).wait_recv()

    if fused:
        per_dev = QH // n
        stats = got[:, per_dev].reshape(n * rows, HD).T
        pieces = []
        for h in range(per_dev):
            c, i = h // (per_dev // 2), h % (per_dev // 2)
            cached = got[:, h].reshape(n * rows, HD).T
            ct, cs = stats[h:h + 1], stats[64 + h:65 + h]
            it, isum = stat[c, me, pl.ds(i, 1), :], stat[c, me, pl.ds(4 + i, 1), :]
            top = jnp.maximum(ct, it)
            ce, ie = jnp.exp(ct - top), jnp.exp(it - top)
            total = cached * ce + num[c, me, pl.ds(i * HD, HD), :] * ie
            pieces.append((total / (cs * ce + isum * ie)).T)
        att = jnp.concatenate(pieces, axis=1).astype(jnp.bfloat16)
    else:
        att = got[...].reshape(n * rows, got.shape[2]).astype(jnp.bfloat16)

    def exchange(c, k):
        m = n >> (k + 1)
        order = orders[c]
        wide = width if m > 1 else width // 2
        half = max(m // 2, 1)
        first = (n - 2 * m) // 2 if m > 1 else n // 2 - 1
        where = (pl.ds(first, half), slice(None), pl.ds(c * width, wide))
        peer = me + (1 - 2 * bit_of(me, order[k])) * (1 << order[k])
        return pltpu.make_async_remote_copy(
            src_ref=sent.at[where], dst_ref=landed.at[where], send_sem=send_sem.at[c, k], recv_sem=recv_sem.at[c, k],
            device_id={"tp": peer}, device_id_type=pl.DeviceIdType.MESH)

    def place(c, k, keep):
        order = orders[c]
        base = 0
        for b in order[:k]:
            base = base + bit_of(me, b) * (1 << b)
        own = bit_of(me, order[k])
        return base + (own if keep else 1 - own) * (1 << order[k]), order[k + 1:]

    def send(c, k):
        m = n >> (k + 1)
        base, rest = place(c, k, False)
        lo = c * width
        cols = pl.ds(lo, width)
        if m > 1:
            first = (n - 2 * m) // 2

            @pl.loop(0, m // 2)
            def _(p):
                a = base + spread(2 * p, rest)
                b = base + spread(2 * p + 1, rest)
                sent[first + p, :, cols] = jnp.concatenate([acc[a, :, cols], acc[b, :, cols]], axis=0).astype(jnp.bfloat16)
        else:
            h = width // 2
            sent[n // 2 - 1, :, pl.ds(lo, h)] = jnp.concatenate(
                [acc[base, :, pl.ds(lo, h)], acc[base, :, pl.ds(lo + h, h)]], axis=0).astype(jnp.bfloat16)
        exchange(c, k).start()

    def receive(c, k):
        m = n >> (k + 1)
        exchange(c, k).wait_recv()
        base, rest = place(c, k, True)
        lo = c * width
        cols = pl.ds(lo, width)
        if m > 1:
            first = (n - 2 * m) // 2

            @pl.loop(0, m // 2)
            def _(p):
                a = base + spread(2 * p, rest)
                b = base + spread(2 * p + 1, rest)
                both = landed[first + p, :, cols].astype(jnp.float32)
                acc[a, :, cols] = acc[a, :, cols] + both[:rows]
                acc[b, :, cols] = acc[b, :, cols] + both[rows:]
        else:
            h = width // 2
            both = landed[n // 2 - 1, :, pl.ds(lo, h)].astype(jnp.float32)
            out_ref[:, pl.ds(lo, h)] = (acc[me, :, pl.ds(lo, h)] + both[:rows]).astype(out_ref.dtype)
            out_ref[:, pl.ds(lo + h, h)] = (acc[me, :, pl.ds(lo + h, h)] + both[rows:]).astype(out_ref.dtype)

    for c in range(CHUNKS):
        loads[c].wait()
        cols = pl.ds(c * width, width)
        acc[:, :, cols] = jnp.dot(att, weight[:, cols], preferred_element_type=jnp.float32).reshape(n, rows, width)
        send(c, 0)
    for k in range(steps):
        for c in range(CHUNKS):
            receive(c, k)
            if k + 1 < steps:
                send(c, k + 1)

    @pl.loop(1, n)
    def _(o):
        att_copy(o).wait_send()

    for copy in started:
        copy.wait_send()
    for k in range(steps):
        for c in range(CHUNKS):
            exchange(c, k).wait_send()


def project(by_owner, out_weight, n, image=()):
    rows = by_owner.shape[0] // 2 if image else by_owner.shape[1]
    model = out_weight.shape[1]
    depth = out_weight.shape[0]
    steps = n.bit_length() - 1
    extra = []
    got = (n, QH // n + 1, rows, HD) if image else by_owner.shape
    if image:
        half = depth // 2
        every = n * rows
        extra = [
            pltpu.VMEM((2, n, half, every), jnp.float32),
            pltpu.VMEM((2, n, 8, every), jnp.float32),
            pltpu.VMEM((2, n - 1, half, every), jnp.bfloat16),
            pltpu.VMEM((2, n - 1, half, every), jnp.bfloat16),
            pltpu.VMEM((2, n - 1, 8, every), jnp.float32),
            pltpu.VMEM((2, n - 1, 8, every), jnp.float32),
            pltpu.SemaphoreType.DMA((2, steps, 2)),
            pltpu.SemaphoreType.DMA((2, steps, 2)),
            pltpu.VMEM(got, jnp.float32),
            pltpu.VMEM((n,) + by_owner.shape, jnp.bfloat16),
            pltpu.VMEM(image[1].shape, jnp.bfloat16),
            pltpu.SemaphoreType.DMA((rows,)),
            pltpu.SemaphoreType.DMA((2, n - 1)),
            pltpu.SemaphoreType.DMA((2, n - 1)),
        ]
    return pl.pallas_call(
        functools.partial(project_kernel, n, bool(image)),
        out_shape=jax.ShapeDtypeStruct((rows, model), jnp.bfloat16),
        in_specs=[pl.BlockSpec(memory_space=pltpu.VMEM), pl.BlockSpec(memory_space=pl.ANY)]
        + [pl.BlockSpec(memory_space=pl.ANY if i == 1 else pltpu.VMEM) for i in range(len(image))],
        out_specs=pl.BlockSpec(memory_space=pltpu.VMEM),
        scratch_shapes=[
            pltpu.VMEM((depth, model), jnp.bfloat16),
            pltpu.VMEM(got, jnp.float32),
            pltpu.VMEM((n, rows, model), jnp.float32),
            pltpu.VMEM((n // 2, 2 * rows, model), jnp.bfloat16),
            pltpu.VMEM((n // 2, 2 * rows, model), jnp.bfloat16),
            pltpu.SemaphoreType.DMA((CHUNKS,)),
            pltpu.SemaphoreType.DMA((n,)),
            pltpu.SemaphoreType.DMA((n,)),
            pltpu.SemaphoreType.DMA((CHUNKS, steps)),
            pltpu.SemaphoreType.DMA((CHUNKS, steps)),
        ] + extra,
        compiler_params=pltpu.CompilerParams(
            collective_id=0, has_side_effects=True, vmem_limit_bytes=48 * 1024 * 1024),
    )(by_owner, out_weight, *image)


def per_device(queries, cache_kv, cache_len, image_kv, row_request, slot_of_request, out_weight):
    tp_size = lax.axis_size("tp")
    my_index = lax.axis_index("tp")
    local_req = queries.shape[0]
    all_req = local_req * tp_size
    img_local = image_kv.shape[0]
    kv_width = KVH * HD
    capacity = max(2, (2 * img_local + all_req - 1) // all_req)
    score_scale = 1.0 / math.sqrt(HD)
    req_iota = jnp.arange(all_req, dtype=jnp.int32)
    my_rows = lax.dynamic_slice_in_dim(row_request[:, 0], my_index * img_local, img_local)
    row_slot = jnp.sum(
        jnp.where(my_rows[:, None] == req_iota[None, :], slot_of_request[None, :], 0), axis=1
    )
    per_dev = QH // tp_size
    if per_dev % 2 == 0 and per_dev <= QH // KVH:
        live = row_slot[:, None] == req_iota[None, :]
        bias = jnp.where(live, 0.0, low_fill).astype(jnp.float32)
        per_group = QH // KVH
        split = queries.reshape(local_req, KVH, 2, per_group // 2 * HD)
        stacked = jnp.transpose(split, (2, 0, 1, 3)).reshape(2 * local_req, QH * HD // 2)
        heads = queries.reshape(local_req, QH, HD).astype(jnp.float32)
        cache_bias = jnp.where(
            jnp.arange(CACHE, dtype=jnp.int32)[None, :] < cache_len[:, None], 0.0, low_fill).astype(jnp.float32)
        return project(stacked, out_weight, tp_size, (heads, cache_kv, cache_bias, image_kv, bias))
    grouped = queries.reshape(local_req, KVH, QH // KVH, HD)
    cache_keys = cache_kv[:, :, :kv_width].reshape(local_req, CACHE, KVH, HD)
    cache_vals = cache_kv[:, :, kv_width:].reshape(local_req, CACHE, KVH, HD)
    cache_scores = (
        jnp.einsum("rgjd,rpgd->rgjp", grouped, cache_keys, preferred_element_type=jnp.float32)
        * score_scale
    )
    cache_live = (jnp.arange(CACHE, dtype=jnp.int32)[None, :] < cache_len[:, None])[
        :, None, None, :
    ]
    cache_top, cache_weights, cache_sum = softmax_part(cache_scores, cache_live, low_fill)
    cache_num = jnp.einsum(
        "rgjp,rpgd->rgjd", cache_weights, cache_vals, preferred_element_type=jnp.float32
    )
    row_iota = jnp.arange(img_local, dtype=jnp.int32)
    earlier = (my_rows[:, None] == my_rows[None, :]) & (row_iota[None, :] < row_iota[:, None])
    row_rank = jnp.sum(earlier.astype(jnp.int32), axis=1)
    bucket = jnp.zeros((all_req * capacity, 2 * kv_width), jnp.bfloat16)
    bucket = bucket.at[row_slot * capacity + row_rank].set(image_kv)
    bucket = bucket.reshape(all_req, capacity, 2 * kv_width)
    arrived = lax.all_to_all(bucket, "tp", split_axis=0, concat_axis=1, tiled=True)
    my_slots = my_index * local_req + jnp.arange(local_req, dtype=jnp.int32)
    owned_slot = slot_of_request[:, None] == my_slots[None, :]
    my_requests = jnp.sum(jnp.where(owned_slot, req_iota[:, None], 0), axis=0)
    matches = (row_request[:, 0][:, None] == my_requests[None, :]).astype(jnp.int32)
    counts = jnp.sum(matches.reshape(tp_size, img_local, local_req), axis=1)
    rank_iota = jnp.arange(capacity, dtype=jnp.int32)
    image_live = rank_iota[None, :, None] < counts[:, None, :]
    image_live = jnp.transpose(image_live, (2, 0, 1)).reshape(local_req, tp_size * capacity)[
        :, None, None, :
    ]
    image_keys = arrived[:, :, :kv_width].reshape(local_req, tp_size * capacity, KVH, HD)
    image_vals = arrived[:, :, kv_width:].reshape(local_req, tp_size * capacity, KVH, HD)
    image_scores = (
        jnp.einsum("rgjd,rsgd->rgjs", grouped, image_keys, preferred_element_type=jnp.float32)
        * score_scale
    )
    image_top, image_weights, image_sum = softmax_part(image_scores, image_live, cache_top)
    image_num = jnp.einsum(
        "rgjs,rsgd->rgjd", image_weights, image_vals, preferred_element_type=jnp.float32
    )
    factor = jnp.exp(cache_top - image_top)
    attended = (cache_num * factor[..., None] + image_num) / (cache_sum * factor + image_sum)[
        ..., None
    ]
    by_owner = jnp.transpose(attended.reshape(local_req, tp_size, QH * HD // tp_size), (1, 0, 2))
    return project(by_owner, out_weight, tp_size)


def solution(mesh):
    placed = (
        P(("groups", "tp"), None),
        P(("groups", "tp"), None, None),
        P(("groups", "tp")),
        P(("groups", "tp"), None),
        P("groups", None),
        P("groups"),
        P("tp", None),
    )
    return jax.shard_map(
        per_device, mesh=mesh, in_specs=placed, out_specs=P(("groups", "tp"), None), check_vma=False
    )
```
